32 devices in a mesh: sec: 4 (over z), row: 4 (over x, core), col: 2 (over y).
Axes of the slice: x: 2, y: 2, z: 4, core: 2. Of those that a mesh axis runs over, the one named last changes fastest.
Arguments:
- amps: bfloat16 [16, 32, 32, 512], P(None, ('sec', 'row'), 'col'), may hold values from -6 to 6
- driver: bfloat16 [16, 32, 32, 512], P(None, 'col', ('sec', 'row')), may hold values from -6 to 6
- ladder_operator: bfloat16 [16384, 16384], P('col', ('sec', 'row')), as said below
- ladder_block_mask: int32 [128, 128], P('col', ('sec', 'row')), may hold values from 0 to 1, as said below
- cycle_op: bfloat16 [16384, 16384], P(('sec', 'row'), 'col'), as said below
- cycle_mask: int32 [128, 128], P(('sec', 'row'), 'col'), may hold values from 0 to 1, as said below
- occ_i: float32 [16], replicated, may hold values from -2 to -0.3
- occ_j: float32 [32], replicated, may hold values from -2 to -0.3
- vir_a: float32 [32], replicated, may hold values from 0.2 to 3
- vir_b: float32 [512], replicated, may hold values from 0.2 to 3
Outputs:
- amp_one: float32 [16, 32, 32, 512], P(None, 'col', ('sec', 'row'))
- amp_two: float32 [16, 32, 32, 512], P(None, ('sec', 'row'), 'col')
The draws below stay inside these ranges and needn't reach their ends.
Inputs may be any that keep to these rules, and one draw needn't show every extreme that they name: ladder_operator is symmetric. cycle_op is symmetric. ladder_block_mask is symmetric with ones on its diagonal. cycle_mask is symmetric with ones on its diagonal.
All inputs are finite; a program needn't handle non-finite values.
Results may differ from the reference program's by a relative error of at most 0.0024.
Values may be sent and summed in bfloat16 or wider, within the bound.
A program may use at most 192 MiB of HBM per device.

```python
import jax
import jax.numpy as jnp

OCCUPIED_FIRST = 16
OCCUPIED_SECOND = 32
VIRTUAL_SLAB = 32
VIRTUAL_COUNT = 512
BLOCK = 128


def symmetric_matrix(key, order):
    raw = jax.random.normal(jax.random.fold_in(key, 11), (order, order), jnp.float32)
    matrix = (raw + raw.T) * 0.7071
    return (matrix * order ** (-0.5)).astype(jnp.bfloat16)


def block_mask(key, count):
    levels = jax.random.randint(jax.random.fold_in(key, 21), (count,), 30, 101)
    raw = jax.random.randint(jax.random.fold_in(key, 22), (count, count), 0, 100)
    places = jnp.arange(count)
    paired = jnp.where(places[:, None] <= places[None, :], raw, raw.T)
    limits = jnp.minimum(levels[:, None], levels[None, :])
    mask = (paired < limits).astype(jnp.int32)
    return jnp.maximum(mask, jnp.eye(count, dtype=jnp.int32))


def draw_ladder_operator(key, part):
    return symmetric_matrix(jax.random.fold_in(key, 1), VIRTUAL_SLAB * VIRTUAL_COUNT)


def draw_cycle_op(key, part):
    return symmetric_matrix(jax.random.fold_in(key, 2), OCCUPIED_SECOND * VIRTUAL_COUNT)


def draw_ladder_block_mask(key, part):
    return block_mask(jax.random.fold_in(key, 3), VIRTUAL_SLAB * VIRTUAL_COUNT // BLOCK)


def draw_cycle_mask(key, part):
    return block_mask(jax.random.fold_in(key, 4), OCCUPIED_SECOND * VIRTUAL_COUNT // BLOCK)


def block_scale(stream_key, shape, pieces, least, largest):
    loudness, own = 1.0, jax.random.fold_in(stream_key, 6)
    for position, blocks in pieces:
        heights = jnp.exp(jax.random.uniform(jax.random.fold_in(own, position), (blocks,), jnp.float32, least / len(pieces), largest / len(pieces)))
        loudness = loudness * jnp.repeat(heights, shape[position] // blocks).reshape([-1 if axis == position else 1 for axis in range(len(shape))])
    return loudness


def bell_draw(own_key, shape, scale, bound, cuts=(), kind=jnp.bfloat16):
    drawn = scale * jax.random.normal(own_key, shape, jnp.float32)
    if cuts:
        drawn = drawn * block_scale(own_key, shape, cuts, -0.22, 0.18)
    return jnp.clip(drawn, -bound, bound).astype(kind)


def setup_inputs(seed: int = 0) -> dict:
    keys = jax.random.split(jax.random.key(seed), 11)
    amps = bell_draw(keys[0], (OCCUPIED_FIRST, OCCUPIED_SECOND, VIRTUAL_SLAB, VIRTUAL_COUNT), 1.0, 6.0, ((1, 16), (2, 2)))
    driver = bell_draw(keys[1], (OCCUPIED_FIRST, OCCUPIED_SECOND, VIRTUAL_SLAB, VIRTUAL_COUNT), 1.0, 6.0, ((1, 2), (2, 16)))
    ladder_operator = draw_ladder_operator(jax.random.fold_in(keys[10], 71), 0)
    ladder_block_mask = draw_ladder_block_mask(jax.random.fold_in(keys[10], 71), 0)
    cycle_op = draw_cycle_op(jax.random.fold_in(keys[10], 71), 0)
    cycle_mask = draw_cycle_mask(jax.random.fold_in(keys[10], 71), 0)
    occ_i = jnp.clip(jax.random.uniform(keys[6], (OCCUPIED_FIRST,), jnp.float32, -2.0, -0.3), -2.0, -0.3)
    occ_j = jnp.clip(jax.random.uniform(keys[7], (OCCUPIED_SECOND,), jnp.float32, -2.0, -0.3), -2.0, -0.3)
    vir_a = jnp.clip(jax.random.uniform(keys[8], (VIRTUAL_SLAB,), jnp.float32, 0.2, 3.0), 0.2, 3.0)
    vir_b = jnp.clip(jax.random.uniform(keys[9], (VIRTUAL_COUNT,), jnp.float32, 0.2, 3.0), 0.2, 3.0)
    return dict(amps=amps, driver=driver, ladder_operator=ladder_operator, ladder_block_mask=ladder_block_mask, cycle_op=cycle_op, cycle_mask=cycle_mask, occ_i=occ_i, occ_j=occ_j, vir_a=vir_a, vir_b=vir_b)


def masked_operator(operator, mask):
    count = mask.shape[0]
    edge = operator.shape[0] // count
    shaped = operator.reshape(count, edge, count, edge)
    return (shaped * mask[:, None, :, None].astype(operator.dtype)).reshape(operator.shape)


def reference(amps, driver, ladder_operator, ladder_block_mask, cycle_op, cycle_mask, occ_i, occ_j, vir_a, vir_b):
    virtual_mask = masked_operator(ladder_operator, ladder_block_mask)
    wmask = masked_operator(cycle_op, cycle_mask)
    denom = (vir_a[None, None, :, None] + vir_b[None, None, None, :]
             - occ_i[:, None, None, None] - occ_j[None, :, None, None])

    def residual(doubles_amplitude):
        ladder_term = jnp.dot(doubles_amplitude.reshape(OCCUPIED_FIRST * OCCUPIED_SECOND, VIRTUAL_SLAB * VIRTUAL_COUNT), virtual_mask, preferred_element_type=jnp.float32)
        ladder_term = ladder_term.reshape(OCCUPIED_FIRST, OCCUPIED_SECOND, VIRTUAL_SLAB, VIRTUAL_COUNT)
        regrouped = jnp.transpose(doubles_amplitude, (0, 2, 1, 3)).reshape(OCCUPIED_FIRST * VIRTUAL_SLAB, OCCUPIED_SECOND * VIRTUAL_COUNT)
        cycle = jnp.dot(regrouped, wmask, preferred_element_type=jnp.float32)
        cycle = jnp.transpose(cycle.reshape(OCCUPIED_FIRST, VIRTUAL_SLAB, OCCUPIED_SECOND, VIRTUAL_COUNT), (0, 2, 1, 3))
        return ladder_term + cycle

    amp_one = (driver.astype(jnp.float32) + residual(amps)) / denom
    amp_rounded = amp_one.astype(jnp.bfloat16)
    amp_two = residual(amp_rounded) / denom
    return amp_one, amp_two
```

```python
import functools

import jax
import jax.numpy as jnp
from jax import lax
from jax.experimental import pallas as pl
from jax.experimental.pallas import tpu as pltpu
from jax.sharding import PartitionSpec as P

MESH = pl.DeviceIdType.MESH


def kernel(
    sizes, x, drv, v_hbm, w_hbm, mv, mw, base, shift_one, shift_two, out_one, out_two,
    va, wa, xa, xb, acca, accb, sa, sb, ra, rb,
    tile_sem, own_sem, ring_s, ring_r, sib_s, sib_r, y_s, y_r, yb_s, yb_r,
    ea_s, ea_r, eb_s, eb_r, ready,
):
    S, R, C = sizes
    W = S * R
    G = W // C
    nch = W // 2
    wide, tall, occ, vir = xa.shape[1:]
    half = tall // 2
    rows = accb.shape[0]
    edge = v_hbm.shape[0] // (mv.shape[0] * mv.shape[1])
    z, row, q = lax.axis_index("sec"), lax.axis_index("row"), lax.axis_index("col")
    me = z * R + row
    core = row % 2
    xchip = row // 2
    p = xchip * S + z + (xchip % 2) * (S - 1 - 2 * z)
    sibling = (z, row + 1 - 2 * core, q)
    home = me // G

    def place(o):
        xo, zo = o // S, o % S
        return xo, zo + (xo % 2) * (S - 1 - 2 * zo)

    def wide_of(o):
        xo, zo = place(o)
        return zo * R + 2 * xo + core

    def device_at(o):
        xo, zo = place(o)
        return (zo, 2 * xo + core, q)

    after, before = device_at((p + 1) % nch), device_at((p + nch - 1) % nch)

    def origin(t, h):
        return (p + nch - t) % nch if h == 0 else (p + t) % nch

    def part(h):
        return pl.ds(h * half, half)

    def remote(src, dst, s, r, device):
        return pltpu.make_async_remote_copy(
            src_ref=src, dst_ref=dst, send_sem=s, recv_sem=r, device_id=device, device_id_type=MESH
        )

    def ring(t, h):
        piece = xa.at[wide_of(origin(t, h)), :, part(h)]
        return remote(piece, piece, ring_s.at[h, t], ring_r.at[h, t], after if h == 0 else before)

    def sib(t, h):
        piece = xa.at[wide_of(origin(t, h)), :, part(h)]
        return remote(piece, piece, sib_s.at[h, t], sib_r.at[h, t], sibling)

    def cross(t, h):
        w = wide_of(origin(t, h))
        goal = w // G
        slot = (q - goal - 1 + C) % C
        return goal, remote(
            xa.at[w, :, part(h)], xb.at[slot, w - goal * G, :, part(h)],
            y_s.at[h, t], y_r.at[slot, h, t], (z, row, goal),
        )

    def cross_in(t, h, slot):
        w = wide_of(origin(t, h))
        piece = xb.at[slot, w - (w // G) * G, :, part(h)]
        return w // G, piece

    barrier = pltpu.get_barrier_semaphore()

    def greet(d, carry):
        w, c = d // C, d % C

        @pl.when(d != me * C + q)
        def _():
            pl.semaphore_signal(barrier, inc=1, device_id=(w // R, w % R, c), device_id_type=MESH)

        return carry

    lax.fori_loop(0, W * C, greet, 0)
    own = pltpu.make_async_copy(x, xa.at[me], own_sem)
    own.start()

    def v_tile(s):
        size = va.shape[1]
        return pltpu.make_async_copy(v_hbm.at[pl.ds(s * size, size), :], va.at[s], tile_sem.at[0, s])

    def w_tile(s):
        size = wa.shape[2]
        return pltpu.make_async_copy(
            w_hbm.at[:, pl.ds(pl.multiple_of(s * size, size), size)], wa.at[s], tile_sem.at[1, s]
        )

    def load(s, carry):
        v_tile(s).start()
        w_tile(s).start()
        return carry

    own.wait()
    pl.semaphore_wait(barrier, W * C - 1)

    def masked(tile, mask, s):
        strips = mask.shape[1]
        for b in range(strips):
            span = pl.ds(b * edge, edge)
            keep = jnp.broadcast_to(mask[s, pl.ds(b, 1), :], (edge, tile.shape[2])).astype(tile.dtype)
            tile[s, span, :] = tile[s, span, :] * keep

    def product(lhs, tile, s, transposed):
        dims = (((1,), (1 if transposed else 0,)), ((), ()))
        return lax.dot_general(lhs, tile[s], dims, preferred_element_type=jnp.float32)

    def gather(sweep):
        def slot_step(t, carry):
            for h in range(2):
                @pl.when(t >= 1)
                def _():
                    ring(t - 1, h).wait_recv()

                @pl.when(t < nch - 1)
                def _():
                    ring(t, h).start()

                sib(t, h).start()
                goal, copy = cross(t, h)

                @pl.when(goal != q)
                def _():
                    copy.start()

            return carry

        lax.fori_loop(0, nch, slot_step, 0)

        def landed(t, carry):
            for h in range(2):
                sib(t, h).wait_recv()
            return carry

        lax.fori_loop(0, nch, landed, 0)

    def pass_on(t):
        for h in range(2):
            for slot in range(C - 1):
                mine, piece = cross_in(t, h, slot)

                @pl.when(mine == q)
                def _():
                    remote(piece, piece, y_s.at[h, t], y_r.at[slot, h, t], sibling).wait_recv()
                    remote(piece, piece, yb_s.at[slot, h, t], yb_r.at[slot, h, t], sibling).start()

    def settle(t, carry):
        for h in range(2):
            for slot in range(C - 1):
                mine, piece = cross_in(t, h, slot)

                @pl.when(mine == q)
                def _():
                    remote(piece, piece, yb_s.at[slot, h, t], yb_r.at[slot, h, t], sibling).wait()

            @pl.when(t < nch - 1)
            def _():
                ring(t, h).wait_send()

            sib(t, h).wait_send()
            goal, copy = cross(t, h)

            @pl.when(goal != q)
            def _():
                copy.wait_send()

        return carry

    def exchange_a(sweep, k):
        return remote(
            sa.at[k - 1], ra.at[sweep, C - 1 - k], ea_s.at[k - 1], ea_r.at[sweep, C - 1 - k], (z, row, (q + k) % C)
        )

    def exchange_b(sweep, k):
        w = (me + k) % W
        block = ((w // G - q + C) % C) * G + w % G
        return w, block, remote(
            sb.at[block], rb.at[sweep, q, me - home * G], eb_s.at[k], eb_r.at[sweep, q, me - home * G], (w // R, w % R, home)
        )

    def sweep_of(sweep, tile_a, tile_b, a_transposed):
        gather(sweep)
        acca[...] = jnp.zeros_like(acca)
        accb[...] = jnp.zeros_like(accb)

        def step_a(s, carry):
            if sweep == 0:
                v_tile(s).wait()
                masked(va, mv, s)
            lhs = xa[:, :, pl.ds(s, 1)].reshape(rows, vir)
            acca[...] += product(lhs, tile_a, s, a_transposed)
            each = -(-nch // tall)
            for e in range(each):
                t = s * each + e

                @pl.when(t < nch)
                def _():
                    pass_on(t)

            return carry

        lax.fori_loop(0, tall, step_a, 0)
        count = rows // C
        for k in range(1, C):
            begin = pl.multiple_of(((q + k) % C) * count, count)
            sa[k - 1] = acca[pl.ds(begin, count), :].astype(sa.dtype)
            exchange_a(sweep, k).start()
        lax.fori_loop(0, nch, settle, 0)

        def step_b(s, carry):
            if sweep == 0:
                w_tile(s).wait()
                masked(wa, mw, s)
            wl, r = s // wide, s % wide
            blocks = [xa[q * G + wl, r].reshape(tall * occ, vir)]
            for slot in range(C - 1):
                blocks.append(xb[slot, wl, r].reshape(tall * occ, vir))
            accb[...] += product(jnp.concatenate(blocks, axis=0), tile_b, s, not a_transposed)
            return carry

        lax.fori_loop(0, tall, step_b, 0)
        if sweep == 0:
            for device in [after, before, sibling] + [(z, row, (q + k) % C) for k in range(1, C)]:
                pl.semaphore_signal(ready, inc=1, device_id=device, device_id_type=MESH)
        sb[...] = accb[...].reshape(sb.shape).astype(sb.dtype)

        def send(k, carry):
            w, block, copy = exchange_b(sweep, k)
            local = jnp.logical_and(w == me, home == q)

            @pl.when(local)
            def _():
                rb[sweep, q, me - home * G] = sb[block]

            @pl.when(jnp.logical_not(local))
            def _():
                copy.start()

            return carry

        lax.fori_loop(0, W, send, 0)
        for k in range(1, C):
            exchange_a(sweep, k).wait()

        def arrive(n, carry):
            c, wl = n // G, n % G

            @pl.when(jnp.logical_or(c != q, q * G + wl != me))
            def _():
                piece = rb.at[sweep, c, wl]
                remote(piece, piece, eb_s.at[0], eb_r.at[sweep, c, wl], sibling).wait_recv()

            return carry

        lax.fori_loop(0, W, arrive, 0)

        def sent(k, carry):
            w, block, copy = exchange_b(sweep, k)

            @pl.when(jnp.logical_not(jnp.logical_and(w == me, home == q)))
            def _():
                copy.wait_send()

            return carry

        lax.fori_loop(0, W, sent, 0)

        def assemble(wl, carry):
            for r in range(wide):
                place_r = wl * wide + r
                for s in range(wide):
                    lanes = pl.ds(s * vir, vir)
                    begin = pl.multiple_of((q * tall + place_r) * occ, occ)
                    total = acca[pl.ds(begin, occ), lanes]
                    for slot in range(C - 1):
                        here = pl.ds(pl.multiple_of(place_r * occ, occ), occ)
                        total += ra[sweep, slot, here, lanes].astype(jnp.float32)
                    for c in range(C):
                        total += rb[sweep, c, wl, pl.ds(s * occ, occ), pl.ds(r * vir, vir)].astype(jnp.float32)
                    if sweep == 0:
                        total += drv[s, place_r].astype(jnp.float32)
                        value = total / (base[...] + shift_one[s, place_r])
                        out_one[s, place_r] = value
                        xa[me, s, place_r] = value.astype(xa.dtype)
                    else:
                        out_two[s, place_r] = total / (base[...] + shift_two[s, place_r])
            return carry

        lax.fori_loop(0, G, assemble, 0)
        if sweep == 0:
            pl.semaphore_wait(ready, C + 2)

    lax.fori_loop(0, tall, load, 0)
    sweep_of(0, va, wa, False)
    sweep_of(1, wa, va, True)


def body(
    amps, driver, ladder_operator, ladder_block_mask, cycle_op, cycle_mask, occ_i, occ_j, vir_a, vir_b,
):
    S, R, C = lax.axis_size("sec"), lax.axis_size("row"), lax.axis_size("col")
    W = S * R
    G = W // C
    nch = W // 2
    wide_index = lax.axis_index(("sec", "row"))
    col_index = lax.axis_index("col")
    occ, wide, tall, vir = amps.shape
    rows = W * wide * occ
    span = wide * vir
    x = jnp.transpose(amps, (1, 2, 0, 3))
    drv = jnp.transpose(driver, (2, 1, 0, 3))
    edge_v = ladder_operator.shape[1] // ladder_block_mask.shape[1]
    edge_w = cycle_op.shape[1] // cycle_mask.shape[1]
    mv = jnp.repeat(ladder_block_mask.astype(jnp.float32), edge_v, axis=1).reshape(tall, -1, span)
    mw = jnp.repeat(cycle_mask.astype(jnp.float32), edge_w, axis=1)
    mw = jnp.transpose(mw.reshape(cycle_mask.shape[0], tall, vir), (1, 0, 2))
    base = vir_b[None, :] - occ_i[:, None]
    shift_one = (
        lax.dynamic_slice_in_dim(vir_a, wide_index * wide, wide)[:, None]
        - lax.dynamic_slice_in_dim(occ_j, col_index * tall, tall)[None, :]
    )
    shift_two = (
        lax.dynamic_slice_in_dim(vir_a, col_index * tall, tall)[None, :]
        - lax.dynamic_slice_in_dim(occ_j, wide_index * wide, wide)[:, None]
    )
    vmem = pl.BlockSpec(memory_space=pltpu.VMEM)
    smem = pl.BlockSpec(memory_space=pltpu.SMEM)
    hbm = pl.BlockSpec(memory_space=pl.ANY)
    dma = pltpu.SemaphoreType.DMA
    half = jnp.bfloat16
    result = jax.ShapeDtypeStruct((wide, tall, occ, vir), jnp.float32)
    one, two = pl.pallas_call(
        functools.partial(kernel, (S, R, C)),
        out_shape=(result, result),
        in_specs=[hbm, vmem, hbm, hbm, vmem, vmem, vmem, smem, smem],
        out_specs=(vmem, vmem),
        scratch_shapes=[
            pltpu.VMEM((tall, vir, span), half),
            pltpu.VMEM((tall, span, vir), half),
            pltpu.VMEM((W, wide, tall, occ, vir), half),
            pltpu.VMEM((C - 1, G, wide, tall, occ, vir), half),
            pltpu.VMEM((rows, span), jnp.float32),
            pltpu.VMEM((rows, span), jnp.float32),
            pltpu.VMEM((C - 1, rows // C, span), half),
            pltpu.VMEM((W, wide * occ, span), half),
            pltpu.VMEM((2, C - 1, rows // C, span), half),
            pltpu.VMEM((2, C, G, wide * occ, span), half),
            dma((2, tall)),
            dma,
            dma((2, nch)),
            dma((2, nch)),
            dma((2, nch)),
            dma((2, nch)),
            dma((2, nch)),
            dma((C - 1, 2, nch)),
            dma((C - 1, 2, nch)),
            dma((C - 1, 2, nch)),
            dma((C - 1,)),
            dma((2, C - 1)),
            dma((W,)),
            dma((2, C, G)),
            pltpu.SemaphoreType.REGULAR,
        ],
        compiler_params=pltpu.CompilerParams(
            collective_id=0, has_side_effects=True, vmem_limit_bytes=63 * 1024 * 1024
        ),
    )(x, drv, ladder_operator, cycle_op, mv, mw, base, shift_one, shift_two)
    return jnp.transpose(one, (2, 1, 0, 3)), jnp.transpose(two, (2, 0, 1, 3))


def solution(mesh):
    placed = (
        P(None, ("sec", "row"), "col", None),
        P(None, "col", ("sec", "row"), None),
        P("col", ("sec", "row")),
        P("col", ("sec", "row")),
        P(("sec", "row"), "col"),
        P(("sec", "row"), "col"),
        P(),
        P(),
        P(),
        P(),
    )
    return jax.shard_map(
        body,
        mesh=mesh,
        in_specs=placed,
        out_specs=(P(None, "col", ("sec", "row"), None), P(None, ("sec", "row"), "col", None)),
        check_vma=False,
    )
```

```python
import functools

import jax
import jax.numpy as jnp
from jax import lax
from jax.experimental import pallas as pl
from jax.experimental.pallas import tpu as pltpu
from jax.sharding import PartitionSpec as P

MESH = pl.DeviceIdType.MESH


def kernel(
    sizes, x, drv, v_hbm, w_hbm, mask_v, mask_w, occ_i, occ_j, vir_a, vir_b, out_one, out_two,
    va, wa, xa, xb, acca, accb, sa, sb, ra, rb, base,
    tile_sem, own_sem, ring_s, ring_r, sib_s, sib_r, y_s, y_r, yb_s, yb_r,
    ea_s, ea_r, eb_s, eb_r, ready,
):
    S, R, C = sizes
    W = S * R
    G = W // C
    nch = W // 2
    wide, tall, occ, vir = xa.shape[1:]
    ways = 2 if wide % 2 == 0 else 1
    half = wide // ways
    near = nch // 2
    block_rows = half * occ
    edge_v = v_hbm.shape[0] // mask_v.shape[0]
    edge_w = w_hbm.shape[0] // mask_w.shape[0]
    z, row, q = lax.axis_index("sec"), lax.axis_index("row"), lax.axis_index("col")
    me = z * R + row
    core = row % 2
    xchip = row // 2
    p = xchip * S + z + (xchip % 2) * (S - 1 - 2 * z)
    sibling = (z, row + 1 - 2 * core, q)
    home = me // G

    def place(o):
        xo, zo = o // S, o % S
        return xo, zo + (xo % 2) * (S - 1 - 2 * zo)

    def wide_of(o, which=None):
        xo, zo = place(o)
        return zo * R + 2 * xo + (core if which is None else which)

    def row_of(w, r):
        zo, ro = w // R, w % R
        xo = ro // 2
        o = xo * S + zo + (xo % 2) * (S - 1 - 2 * zo)
        h, rest = r // half, r % half
        d = (p - o + nch) % nch if h == 0 else (o - p + nch) % nch
        index = (((d // near) * ways + h) * near + d % near) * 2 + ro % 2
        return pl.multiple_of(index * block_rows + rest * occ, occ)

    def device_at(o):
        xo, zo = place(o)
        return (zo, 2 * xo + core, q)

    after, before = device_at((p + 1) % nch), device_at((p + nch - 1) % nch)

    def origin(t, h):
        return (p + nch - t) % nch if h == 0 else (p + t) % nch

    def part(h):
        return pl.ds(h * half, half)

    def remote(src, dst, s, r, device):
        return pltpu.make_async_remote_copy(
            src_ref=src, dst_ref=dst, send_sem=s, recv_sem=r, device_id=device, device_id_type=MESH
        )

    def ring(t, h):
        piece = xa.at[wide_of(origin(t, h)), part(h)]
        return remote(piece, piece, ring_s.at[h, t], ring_r.at[h, t], after if h == 0 else before)

    def sib(t, h):
        piece = xa.at[wide_of(origin(t, h)), part(h)]
        return remote(piece, piece, sib_s.at[h, t], sib_r.at[h, t], sibling)

    def cross(t, h):
        w = wide_of(origin(t, h))
        goal = w // G
        slot = (q - goal - 1 + C) % C
        return goal, remote(
            xa.at[w, part(h)], xb.at[slot, w - goal * G, part(h)],
            y_s.at[h, t], y_r.at[slot, h, t], (z, row, goal),
        )

    def cross_in(t, h, slot):
        w = wide_of(origin(t, h))
        piece = xb.at[slot, w - (w // G) * G, part(h)]
        return w // G, piece

    barrier = pltpu.get_barrier_semaphore()

    def greet(d, carry):
        w, c = d // C, d % C

        @pl.when(d != me * C + q)
        def _():
            pl.semaphore_signal(barrier, inc=1, device_id=(w // R, w % R, c), device_id_type=MESH)

        return carry

    lax.fori_loop(0, W * C, greet, 0)
    own = pltpu.make_async_copy(x, xa.at[me], own_sem)
    own.start()

    def v_tile(s):
        size = va.shape[1]
        return pltpu.make_async_copy(v_hbm.at[pl.ds(s * size, size), :], va.at[s], tile_sem.at[0, s])

    def w_tile(s):
        size = wa.shape[2]
        return pltpu.make_async_copy(
            w_hbm.at[:, pl.ds(pl.multiple_of(s * size, size), size)], wa.at[s], tile_sem.at[1, s]
        )

    def load(s, carry):
        v_tile(s).start()
        w_tile(s).start()
        return carry

    own.wait()
    pl.semaphore_wait(barrier, W * C - 1)

    def cover(tile, s, rows, lanes, keep):
        keep = jnp.full((rows.size, lanes.size), keep.astype(jnp.float32)).astype(tile.dtype)
        tile[s, rows, lanes] = tile[s, rows, lanes] * keep

    def mask_tiles(s):
        strips, across = va.shape[1] // edge_v, va.shape[2] // edge_v
        v_tile(s).wait()
        for b in range(strips):
            for c in range(across):
                cover(va, s, pl.ds(b * edge_v, edge_v), pl.ds(c * edge_v, edge_v), mask_v[s * strips + b, c])
        strips, across = wa.shape[1] // edge_w, wa.shape[2] // edge_w
        w_tile(s).wait()
        for b in range(strips):
            for c in range(across):
                cover(wa, s, pl.ds(b * edge_w, edge_w), pl.ds(c * edge_w, edge_w), mask_w[b, s * across + c])

    def product(lhs, tile, s, transposed):
        dims = (((1,), (1 if transposed else 0,)), ((), ()))
        return lax.dot_general(lhs, tile[s], dims, preferred_element_type=jnp.float32)

    def step_a(far, tile, s, transposed):
        blocks = []
        for h in range(ways):
            for d in range(near):
                o = origin(far * near + d, h)
                for which in range(2):
                    piece = xa[wide_of(o, which), pl.ds(h * half, half), pl.ds(s, 1)]
                    blocks.append(piece.reshape(block_rows, vir))
        count = len(blocks) * block_rows
        span = pl.ds(far * count, count)
        acca[span, :] += product(jnp.concatenate(blocks, axis=0), tile, s, transposed)

    def unit_b(source, wl, h, slot, tile, transposed):
        for rest in range(half):
            r = h * half + rest
            lhs = source[r].reshape(tall * occ, vir)
            accb[slot] += product(lhs, tile, wl * wide + r, transposed)

    def own_units(t, tile, transposed):
        for h in range(ways):
            w = wide_of(origin(t, h), 0)

            @pl.when(w // G == q)
            def _():
                for which in range(2):
                    unit_b(xa.at[w + which], w + which - q * G, h, 0, tile, transposed)

    def cross_units(t, tile, transposed):
        for h in range(ways):
            w = wide_of(origin(t, h), 0)

            @pl.when(w // G == q)
            def _():
                for slot in range(C - 1):
                    wl = w + core - q * G
                    unit_b(xb.at[slot, wl], wl, h, 1 + slot, tile, transposed)
                    wl = w + 1 - core - q * G
                    piece = xb.at[slot, wl, part(h)]
                    remote(piece, piece, yb_s.at[slot, h, t], yb_r.at[slot, h, t], sibling).wait_recv()
                    unit_b(xb.at[slot, wl], wl, h, 1 + slot, tile, transposed)

    def gather(sweep, tile_a, tile_b, a_transposed):
        each = -(-tall // near)

        def slot_step(t, carry):
            for h in range(ways):
                @pl.when(t >= 1)
                def _():
                    ring(t - 1, h).wait_recv()

                @pl.when(t < nch - 1)
                def _():
                    ring(t, h).start()

                sib(t, h).start()
                goal, copy = cross(t, h)

                @pl.when(goal != q)
                def _():
                    copy.start()

            @pl.when(t >= 1)
            def _():
                for h in range(ways):
                    sib(t - 1, h).wait_recv()

            def work(n, carry):
                s = (t % near) * each + n

                @pl.when(s < tall)
                def _():
                    if sweep == 0:
                        @pl.when(t < near)
                        def _():
                            mask_tiles(s)

                    @pl.when(t >= near)
                    def _():
                        step_a(0, tile_a, s, a_transposed)

                return carry

            lax.fori_loop(0, each, work, 0)

            def pair(n, carry):
                d = 2 * (t - near) + n

                @pl.when(jnp.logical_and(d >= 0, d < t))
                def _():
                    own_units(d, tile_b, not a_transposed)

                return carry

            lax.fori_loop(0, 2, pair, 0)
            return carry

        lax.fori_loop(0, nch, slot_step, 0)
        for h in range(ways):
            sib(nch - 1, h).wait_recv()
        own_units(nch - 1, tile_b, not a_transposed)

    def pass_on(t):
        for h in range(ways):
            for slot in range(C - 1):
                mine, piece = cross_in(t, h, slot)

                @pl.when(mine == q)
                def _():
                    remote(piece, piece, y_s.at[h, t], y_r.at[slot, h, t], sibling).wait_recv()
                    remote(piece, piece, yb_s.at[slot, h, t], yb_r.at[slot, h, t], sibling).start()

    def settle(t, carry):
        for h in range(ways):
            for slot in range(C - 1):
                mine, piece = cross_in(t, h, slot)

                @pl.when(mine == q)
                def _():
                    remote(piece, piece, yb_s.at[slot, h, t], yb_r.at[slot, h, t], sibling).wait_send()

            @pl.when(t < nch - 1)
            def _():
                ring(t, h).wait_send()

            sib(t, h).wait_send()
            goal, copy = cross(t, h)

            @pl.when(goal != q)
            def _():
                copy.wait_send()

        return carry

    def exchange_a(sweep, k):
        return remote(
            sa.at[k - 1], ra.at[sweep, C - 1 - k], ea_s.at[k - 1], ea_r.at[sweep, C - 1 - k], (z, row, (q + k) % C)
        )

    def exchange_b(sweep, k):
        w = (me + k) % W
        block = ((w // G - q + C) % C) * G + w % G
        return w, block, remote(
            sb.at[block], rb.at[sweep, q, me - home * G], eb_s.at[k], eb_r.at[sweep, q, me - home * G], (w // R, w % R, home)
        )

    def sweep_of(sweep, tile_a, tile_b, a_transposed):
        acca[...] = jnp.zeros_like(acca)
        accb[...] = jnp.zeros_like(accb)
        gather(sweep, tile_a, tile_b, a_transposed)

        def rest_a(s, carry):
            step_a(1, tile_a, s, a_transposed)
            return carry

        lax.fori_loop(0, tall, rest_a, 0)

        def arrivals(t, carry):
            pass_on(t)

            @pl.when(t >= 1)
            def _():
                cross_units(t - 1, tile_b, not a_transposed)

            return carry

        lax.fori_loop(0, nch, arrivals, 0)
        for k in range(1, C):
            def fill(wl, carry):
                for r in range(wide):
                    here = pl.ds(pl.multiple_of((wl * wide + r) * occ, occ), occ)
                    there = pl.ds(row_of(((q + k) % C) * G + wl, r), occ)
                    sa[k - 1, here, :] = acca[there, :].astype(sa.dtype)
                return carry

            lax.fori_loop(0, G, fill, 0)
            exchange_a(sweep, k).start()
        cross_units(nch - 1, tile_b, not a_transposed)
        lax.fori_loop(0, nch, settle, 0)
        if sweep == 0:
            for device in [after, before, sibling] + [(z, row, (q + k) % C) for k in range(1, C)]:
                pl.semaphore_signal(ready, inc=1, device_id=device, device_id_type=MESH)
        sb[...] = accb[...].reshape(sb.shape).astype(sb.dtype)

        def send(k, carry):
            w, block, copy = exchange_b(sweep, k)
            local = jnp.logical_and(w == me, home == q)

            @pl.when(local)
            def _():
                rb[sweep, q, me - home * G] = sb[block]

            @pl.when(jnp.logical_not(local))
            def _():
                copy.start()

            return carry

        lax.fori_loop(0, W, send, 0)
        for k in range(1, C):
            exchange_a(sweep, k).wait()

        def arrive(n, carry):
            c, wl = n // G, n % G

            @pl.when(jnp.logical_or(c != q, q * G + wl != me))
            def _():
                piece = rb.at[sweep, c, wl]
                remote(piece, piece, eb_s.at[0], eb_r.at[sweep, c, wl], sibling).wait_recv()

            return carry

        lax.fori_loop(0, W, arrive, 0)

        def sent(k, carry):
            w, block, copy = exchange_b(sweep, k)

            @pl.when(jnp.logical_not(jnp.logical_and(w == me, home == q)))
            def _():
                copy.wait_send()

            return carry

        lax.fori_loop(0, W, sent, 0)

        def assemble(wl, carry):
            for r in range(wide):
                place_r = wl * wide + r
                for s in range(wide):
                    lanes = pl.ds(s * vir, vir)
                    total = acca[pl.ds(row_of(q * G + wl, r), occ), lanes]
                    for slot in range(C - 1):
                        here = pl.ds(pl.multiple_of(place_r * occ, occ), occ)
                        total += ra[sweep, slot, here, lanes].astype(jnp.float32)
                    for c in range(C):
                        total += rb[sweep, c, wl, pl.ds(s * occ, occ), pl.ds(r * vir, vir)].astype(jnp.float32)
                    if sweep == 0:
                        total += drv[s, place_r].astype(jnp.float32)
                        value = total / (base[...] + (vir_a[me * wide + s] - occ_j[q * tall + place_r]))
                        out_one[s, place_r] = value
                        xa[me, s, place_r] = value.astype(xa.dtype)
                    else:
                        out_two[s, place_r] = total / (base[...] + (vir_a[q * tall + place_r] - occ_j[me * wide + s]))
            return carry

        lax.fori_loop(0, G, assemble, 0)
        if sweep == 0:
            pl.semaphore_wait(ready, C + 2)

    lax.fori_loop(0, tall, load, 0)
    for i in range(occ):
        base[pl.ds(i, 1), :] = vir_b[...] - occ_i[i]
    sweep_of(0, va, wa, False)
    sweep_of(1, wa, va, True)


def body(
    amps, driver, ladder_operator, ladder_block_mask, cycle_op, cycle_mask, occ_i, occ_j, vir_a, vir_b,
):
    S, R, C = lax.axis_size("sec"), lax.axis_size("row"), lax.axis_size("col")
    W = S * R
    G = W // C
    nch = W // 2
    occ, wide, tall, vir = amps.shape
    rows = W * wide * occ
    span = wide * vir
    x = jnp.transpose(amps, (1, 2, 0, 3))
    drv = jnp.transpose(driver, (2, 1, 0, 3))
    vmem = pl.BlockSpec(memory_space=pltpu.VMEM)
    smem = pl.BlockSpec(memory_space=pltpu.SMEM)
    hbm = pl.BlockSpec(memory_space=pl.ANY)
    dma = pltpu.SemaphoreType.DMA
    half = jnp.bfloat16
    result = jax.ShapeDtypeStruct((wide, tall, occ, vir), jnp.float32)
    one, two = pl.pallas_call(
        functools.partial(kernel, (S, R, C)),
        out_shape=(result, result),
        in_specs=[hbm, vmem, hbm, hbm, smem, smem, smem, smem, smem, vmem],
        out_specs=(vmem, vmem),
        scratch_shapes=[
            pltpu.VMEM((tall, vir, span), half),
            pltpu.VMEM((tall, span, vir), half),
            pltpu.VMEM((W, wide, tall, occ, vir), half),
            pltpu.VMEM((C - 1, G, wide, tall, occ, vir), half),
            pltpu.VMEM((rows, span), jnp.float32),
            pltpu.VMEM((C, tall * occ, span), jnp.float32),
            pltpu.VMEM((C - 1, rows // C, span), half),
            pltpu.VMEM((W, wide * occ, span), half),
            pltpu.VMEM((2, C - 1, rows // C, span), half),
            pltpu.VMEM((2, C, G, wide * occ, span), half),
            pltpu.VMEM((occ, vir), jnp.float32),
            dma((2, tall)),
            dma,
            dma((2, nch)),
            dma((2, nch)),
            dma((2, nch)),
            dma((2, nch)),
            dma((2, nch)),
            dma((C - 1, 2, nch)),
            dma((C - 1, 2, nch)),
            dma((C - 1, 2, nch)),
            dma((C - 1,)),
            dma((2, C - 1)),
            dma((W,)),
            dma((2, C, G)),
            pltpu.SemaphoreType.REGULAR,
        ],
        compiler_params=pltpu.CompilerParams(
            collective_id=0, has_side_effects=True, vmem_limit_bytes=63 * 1024 * 1024
        ),
    )(x, drv, ladder_operator, cycle_op, ladder_block_mask, cycle_mask, occ_i, occ_j, vir_a, vir_b[None])
    return jnp.transpose(one, (2, 1, 0, 3)), jnp.transpose(two, (2, 0, 1, 3))


def solution(mesh):
    placed = (
        P(None, ("sec", "row"), "col", None),
        P(None, "col", ("sec", "row"), None),
        P("col", ("sec", "row")),
        P("col", ("sec", "row")),
        P(("sec", "row"), "col"),
        P(("sec", "row"), "col"),
        P(),
        P(),
        P(),
        P(),
    )
    return jax.shard_map(
        body,
        mesh=mesh,
        in_specs=placed,
        out_specs=(P(None, "col", ("sec", "row"), None), P(None, ("sec", "row"), "col", None)),
        check_vma=False,
    )
```

```python
import functools

import jax
import jax.numpy as jnp
from jax import lax
from jax.experimental import pallas as pl
from jax.experimental.pallas import tpu as pltpu
from jax.sharding import PartitionSpec as P

MESH = pl.DeviceIdType.MESH


def kernel(
    sizes, x, drv, v_hbm, w_hbm, mask_v, mask_w, occ_i, occ_j, vir_a, vir_b, out_one, out_two,
    va, wa, xa, xb, acca, accb, sa, sb, ra, rb, base,
    tile_sem, own_sem, ring_s, ring_r, sib_s, sib_r, y_s, y_r, yb_s, yb_r,
    ea_s, ea_r, eb_s, eb_r, ready,
):
    S, R, C = sizes
    W = S * R
    G = W // C
    nch = W // 2
    wide, tall, occ, vir = xa.shape[1:]
    ways = 2 if wide % 2 == 0 else 1
    half = wide // ways
    near = nch // 2
    block_rows = half * occ
    edge_v = v_hbm.shape[0] // mask_v.shape[0]
    edge_w = w_hbm.shape[0] // mask_w.shape[0]
    z, row, q = lax.axis_index("sec"), lax.axis_index("row"), lax.axis_index("col")
    me = z * R + row
    core = row % 2
    xchip = row // 2
    p = xchip * S + z + (xchip % 2) * (S - 1 - 2 * z)
    sibling = (z, row + 1 - 2 * core, q)

    def place(o):
        xo, zo = o // S, o % S
        return xo, zo + (xo % 2) * (S - 1 - 2 * zo)

    def wide_of(o, which=None):
        xo, zo = place(o)
        return zo * R + 2 * xo + (core if which is None else which)

    def row_of(w, r):
        zo, ro = w // R, w % R
        xo = ro // 2
        o = xo * S + zo + (xo % 2) * (S - 1 - 2 * zo)
        h, rest = r // half, r % half
        d = (p - o + nch) % nch if h == 0 else (o - p + nch) % nch
        index = (((d // near) * ways + h) * near + d % near) * 2 + ro % 2
        return pl.multiple_of(index * block_rows + rest * occ, occ)

    def device_at(o):
        xo, zo = place(o)
        return (zo, 2 * xo + core, q)

    after, before = device_at((p + 1) % nch), device_at((p + nch - 1) % nch)

    def origin(t, h):
        return (p + nch - t) % nch if h == 0 else (p + t) % nch

    def part(h):
        return pl.ds(h * half, half)

    def remote(src, dst, s, r, device):
        return pltpu.make_async_remote_copy(
            src_ref=src, dst_ref=dst, send_sem=s, recv_sem=r, device_id=device, device_id_type=MESH
        )

    def ring(t, h):
        piece = xa.at[wide_of(origin(t, h)), part(h)]
        return remote(piece, piece, ring_s.at[h, t], ring_r.at[h, t], after if h == 0 else before)

    def sib(t, h):
        piece = xa.at[wide_of(origin(t, h)), part(h)]
        return remote(piece, piece, sib_s.at[h, t], sib_r.at[h, t], sibling)

    def cross(t, h):
        w = wide_of(origin(t, h))
        goal = w // G
        slot = (q - goal - 1 + C) % C
        return goal, remote(
            xa.at[w, part(h)], xb.at[slot, w - goal * G, part(h)],
            y_s.at[h, t], y_r.at[slot, h, t], (z, row, goal),
        )

    def cross_in(t, h, slot):
        w = wide_of(origin(t, h))
        piece = xb.at[slot, w - (w // G) * G, part(h)]
        return w // G, piece

    barrier = pltpu.get_barrier_semaphore()

    def greet(d, carry):
        w, c = d // C, d % C

        @pl.when(d != me * C + q)
        def _():
            pl.semaphore_signal(barrier, inc=1, device_id=(w // R, w % R, c), device_id_type=MESH)

        return carry

    lax.fori_loop(0, W * C, greet, 0)
    own = pltpu.make_async_copy(x, xa.at[me], own_sem)
    own.start()

    def v_tile(s):
        size = va.shape[1]
        return pltpu.make_async_copy(v_hbm.at[pl.ds(s * size, size), :], va.at[s], tile_sem.at[0, s])

    def w_tile(s):
        size = wa.shape[2]
        return pltpu.make_async_copy(
            w_hbm.at[:, pl.ds(pl.multiple_of(s * size, size), size)], wa.at[s], tile_sem.at[1, s]
        )

    def load(s, carry):
        v_tile(s).start()
        w_tile(s).start()
        return carry

    own.wait()
    pl.semaphore_wait(barrier, W * C - 1)

    def cover(tile, s, rows, lanes, keep):
        keep = jnp.full((rows.size, lanes.size), keep.astype(jnp.float32)).astype(tile.dtype)
        tile[s, rows, lanes] = tile[s, rows, lanes] * keep

    def mask_tiles(s):
        strips, across = va.shape[1] // edge_v, va.shape[2] // edge_v
        v_tile(s).wait()
        for b in range(strips):
            for c in range(across):
                cover(va, s, pl.ds(b * edge_v, edge_v), pl.ds(c * edge_v, edge_v), mask_v[s * strips + b, c])
        strips, across = wa.shape[1] // edge_w, wa.shape[2] // edge_w
        w_tile(s).wait()
        for b in range(strips):
            for c in range(across):
                cover(wa, s, pl.ds(b * edge_w, edge_w), pl.ds(c * edge_w, edge_w), mask_w[b, s * across + c])

    def product(lhs, tile, s, transposed):
        dims = (((1,), (1 if transposed else 0,)), ((), ()))
        return lax.dot_general(lhs, tile[s], dims, preferred_element_type=jnp.float32)

    def step_a(far, tile, s, transposed):
        blocks = []
        for h in range(ways):
            for d in range(near):
                o = origin(far * near + d, h)
                for which in range(2):
                    piece = xa[wide_of(o, which), pl.ds(h * half, half), pl.ds(s, 1)]
                    blocks.append(piece.reshape(block_rows, vir))
        count = len(blocks) * block_rows
        span = pl.ds(far * count, count)
        acca[span, :] += product(jnp.concatenate(blocks, axis=0), tile, s, transposed)

    def unit_b(source, wl, h, slot, tile, transposed):
        for rest in range(half):
            r = h * half + rest
            lhs = source[r].reshape(tall * occ, vir)
            accb[slot] += product(lhs, tile, wl * wide + r, transposed)

    def own_units(t, tile, transposed):
        for h in range(ways):
            w = wide_of(origin(t, h), 0)

            @pl.when(w // G == q)
            def _():
                for which in range(2):
                    unit_b(xa.at[w + which], w + which - q * G, h, 0, tile, transposed)

    def cross_units(t, tile, transposed):
        for h in range(ways):
            w = wide_of(origin(t, h), 0)

            @pl.when(w // G == q)
            def _():
                for slot in range(C - 1):
                    wl = w + core - q * G
                    unit_b(xb.at[slot, wl], wl, h, 1 + slot, tile, transposed)
                    wl = w + 1 - core - q * G
                    piece = xb.at[slot, wl, part(h)]
                    remote(piece, piece, yb_s.at[slot, h, t], yb_r.at[slot, h, t], sibling).wait_recv()
                    unit_b(xb.at[slot, wl], wl, h, 1 + slot, tile, transposed)

    def gather(sweep, tile_a, tile_b, a_transposed):
        each = -(-tall // near)

        def slot_step(t, carry):
            for h in range(ways):
                @pl.when(t >= 1)
                def _():
                    ring(t - 1, h).wait_recv()

                @pl.when(t < nch - 1)
                def _():
                    ring(t, h).start()

                sib(t, h).start()
                goal, copy = cross(t, h)

                @pl.when(goal != q)
                def _():
                    copy.start()

            @pl.when(t >= 1)
            def _():
                for h in range(ways):
                    sib(t - 1, h).wait_recv()

            def work(n, carry):
                s = (t % near) * each + n

                @pl.when(s < tall)
                def _():
                    if sweep == 0:
                        @pl.when(t < near)
                        def _():
                            mask_tiles(s)

                    @pl.when(t >= near)
                    def _():
                        step_a(0, tile_a, s, a_transposed)

                return carry

            lax.fori_loop(0, each, work, 0)

            def pair(n, carry):
                d = 2 * (t - near) + n

                @pl.when(jnp.logical_and(d >= 0, d < t))
                def _():
                    own_units(d, tile_b, not a_transposed)

                return carry

            lax.fori_loop(0, 2, pair, 0)
            return carry

        lax.fori_loop(0, nch, slot_step, 0)
        for h in range(ways):
            sib(nch - 1, h).wait_recv()
        own_units(nch - 1, tile_b, not a_transposed)

    def pass_on(t):
        for h in range(ways):
            for slot in range(C - 1):
                mine, piece = cross_in(t, h, slot)

                @pl.when(mine == q)
                def _():
                    remote(piece, piece, y_s.at[h, t], y_r.at[slot, h, t], sibling).wait_recv()
                    remote(piece, piece, yb_s.at[slot, h, t], yb_r.at[slot, h, t], sibling).start()

    def settle(t, carry):
        for h in range(ways):
            for slot in range(C - 1):
                mine, piece = cross_in(t, h, slot)

                @pl.when(mine == q)
                def _():
                    remote(piece, piece, yb_s.at[slot, h, t], yb_r.at[slot, h, t], sibling).wait_send()

            @pl.when(t < nch - 1)
            def _():
                ring(t, h).wait_send()

            sib(t, h).wait_send()
            goal, copy = cross(t, h)

            @pl.when(goal != q)
            def _():
                copy.wait_send()

        return carry

    def exchange_a(sweep, k, wl):
        return remote(
            sa.at[k - 1, wl], ra.at[sweep, C - 1 - k, wl],
            ea_s.at[k - 1, wl], ea_r.at[sweep, C - 1 - k, wl], (z, row, (q + k) % C),
        )

    def exchange_b(sweep, k):
        w = (me + k) % W
        block = ((w // G - q + C) % C) * G + w % G
        return block, remote(
            sb.at[block], rb.at[sweep, me], eb_s.at[k], eb_r.at[sweep, me], (w // R, w % R, q)
        )

    def arrive(sweep, w):
        @pl.when(w != me)
        def _():
            piece = rb.at[sweep, w]
            remote(piece, piece, eb_s.at[0], eb_r.at[sweep, w], sibling).wait_recv()

    def plane_sum(sweep, w, r, s):
        lanes = pl.ds(s * vir, vir)
        both = acca[pl.ds(row_of(w, r), occ), lanes]
        return both + rb[sweep, w, pl.ds(s * occ, occ), pl.ds(r * vir, vir)].astype(jnp.float32)

    def sweep_of(sweep, tile_a, tile_b, a_transposed):
        acca[...] = jnp.zeros_like(acca)
        accb[...] = jnp.zeros_like(accb)
        gather(sweep, tile_a, tile_b, a_transposed)

        def rest_a(s, carry):
            step_a(1, tile_a, s, a_transposed)
            return carry

        lax.fori_loop(0, tall, rest_a, 0)

        def arrivals(t, carry):
            pass_on(t)

            @pl.when(t >= 1)
            def _():
                cross_units(t - 1, tile_b, not a_transposed)

            return carry

        lax.fori_loop(0, nch, arrivals, 0)
        cross_units(nch - 1, tile_b, not a_transposed)
        lax.fori_loop(0, nch, settle, 0)
        if sweep == 0:
            for device in [after, before, sibling] + [(z, row, (q + k) % C) for k in range(1, C)]:
                pl.semaphore_signal(ready, inc=1, device_id=device, device_id_type=MESH)
        sb[...] = accb[...].reshape(sb.shape).astype(sb.dtype)

        rb[sweep, me] = sb[me % G + ((me // G - q + C) % C) * G]

        def send(k, carry):
            exchange_b(sweep, k)[1].start()
            return carry

        lax.fori_loop(1, W, send, 0)
        for k in range(1, C):
            def fill(wl, carry):
                w = ((q + k) % C) * G + wl
                arrive(sweep, w)
                for r in range(wide):
                    for s in range(wide):
                        sa[k - 1, wl, pl.ds(r * occ, occ), pl.ds(s * vir, vir)] = plane_sum(sweep, w, r, s).astype(sa.dtype)
                exchange_a(sweep, k, wl).start()
                return carry

            lax.fori_loop(0, G, fill, 0)

        def assemble(wl, carry):
            arrive(sweep, q * G + wl)
            for k in range(1, C):
                exchange_a(sweep, k, wl).wait()
            for r in range(wide):
                place_r = wl * wide + r
                for s in range(wide):
                    total = plane_sum(sweep, q * G + wl, r, s)
                    for slot in range(C - 1):
                        total += ra[sweep, slot, wl, pl.ds(r * occ, occ), pl.ds(s * vir, vir)].astype(jnp.float32)
                    if sweep == 0:
                        total += drv[s, place_r].astype(jnp.float32)
                        value = total / (base[...] + (vir_a[me * wide + s] - occ_j[q * tall + place_r]))
                        out_one[s, place_r] = value
                        xa[me, s, place_r] = value.astype(xa.dtype)
                    else:
                        out_two[s, place_r] = total / (base[...] + (vir_a[q * tall + place_r] - occ_j[me * wide + s]))
            return carry

        lax.fori_loop(0, G, assemble, 0)

        def sent(k, carry):
            exchange_b(sweep, k)[1].wait_send()
            return carry

        lax.fori_loop(1, W, sent, 0)
        if sweep == 0:
            pl.semaphore_wait(ready, C + 2)

    lax.fori_loop(0, tall, load, 0)
    for i in range(occ):
        base[pl.ds(i, 1), :] = vir_b[...] - occ_i[i]
    sweep_of(0, va, wa, False)
    sweep_of(1, wa, va, True)


def body(
    amps, driver, ladder_operator, ladder_block_mask, cycle_op, cycle_mask, occ_i, occ_j, vir_a, vir_b,
):
    S, R, C = lax.axis_size("sec"), lax.axis_size("row"), lax.axis_size("col")
    W = S * R
    G = W // C
    nch = W // 2
    occ, wide, tall, vir = amps.shape
    rows = W * wide * occ
    span = wide * vir
    x = jnp.transpose(amps, (1, 2, 0, 3))
    drv = jnp.transpose(driver, (2, 1, 0, 3))
    vmem = pl.BlockSpec(memory_space=pltpu.VMEM)
    smem = pl.BlockSpec(memory_space=pltpu.SMEM)
    hbm = pl.BlockSpec(memory_space=pl.ANY)
    dma = pltpu.SemaphoreType.DMA
    half = jnp.bfloat16
    result = jax.ShapeDtypeStruct((wide, tall, occ, vir), jnp.float32)
    one, two = pl.pallas_call(
        functools.partial(kernel, (S, R, C)),
        out_shape=(result, result),
        in_specs=[hbm, vmem, hbm, hbm, smem, smem, smem, smem, smem, vmem],
        out_specs=(vmem, vmem),
        scratch_shapes=[
            pltpu.VMEM((tall, vir, span), half),
            pltpu.VMEM((tall, span, vir), half),
            pltpu.VMEM((W, wide, tall, occ, vir), half),
            pltpu.VMEM((C - 1, G, wide, tall, occ, vir), half),
            pltpu.VMEM((rows, span), jnp.float32),
            pltpu.VMEM((C, tall * occ, span), jnp.float32),
            pltpu.VMEM((C - 1, G, wide * occ, span), half),
            pltpu.VMEM((W, wide * occ, span), half),
            pltpu.VMEM((2, C - 1, G, wide * occ, span), half),
            pltpu.VMEM((2, W, wide * occ, span), half),
            pltpu.VMEM((occ, vir), jnp.float32),
            dma((2, tall)),
            dma,
            dma((2, nch)),
            dma((2, nch)),
            dma((2, nch)),
            dma((2, nch)),
            dma((2, nch)),
            dma((C - 1, 2, nch)),
            dma((C - 1, 2, nch)),
            dma((C - 1, 2, nch)),
            dma((C - 1, G)),
            dma((2, C - 1, G)),
            dma((W,)),
            dma((2, W)),
            pltpu.SemaphoreType.REGULAR,
        ],
        compiler_params=pltpu.CompilerParams(
            collective_id=0, has_side_effects=True, vmem_limit_bytes=63 * 1024 * 1024
        ),
    )(x, drv, ladder_operator, cycle_op, ladder_block_mask, cycle_mask, occ_i, occ_j, vir_a, vir_b[None])
    return jnp.transpose(one, (2, 1, 0, 3)), jnp.transpose(two, (2, 0, 1, 3))


def solution(mesh):
    placed = (
        P(None, ("sec", "row"), "col", None),
        P(None, "col", ("sec", "row"), None),
        P("col", ("sec", "row")),
        P("col", ("sec", "row")),
        P(("sec", "row"), "col"),
        P(("sec", "row"), "col"),
        P(),
        P(),
        P(),
        P(),
    )
    return jax.shard_map(
        body,
        mesh=mesh,
        in_specs=placed,
        out_specs=(P(None, "col", ("sec", "row"), None), P(None, ("sec", "row"), "col", None)),
        check_vma=False,
    )
```

```python
import functools

import jax
import jax.numpy as jnp
from jax import lax
from jax.experimental import pallas as pl
from jax.experimental.pallas import tpu as pltpu
from jax.sharding import PartitionSpec as P

MESH = pl.DeviceIdType.MESH


def kernel(
    sizes, x, drv, v_hbm, w_hbm, mask_v, mask_w, occ_i, occ_j, vir_a, vir_b, out_one, out_two,
    va, wa, xa, xb, acca, accb, sa, sb, ra, rb, base,
    tile_sem, own_sem, ring_s, ring_r, sib_s, sib_r, y_s, y_r, yb_s, yb_r,
    ea_s, ea_r, eb_s, eb_r, ready,
):
    S, R, C = sizes
    W = S * R
    G = W // C
    nch = W // 2
    wide, tall, occ, vir = xa.shape[1:]
    ways = 2 if wide % 2 == 0 else 1
    half = wide // ways
    near = nch // 2
    block_rows = half * occ
    edge_v = v_hbm.shape[0] // mask_v.shape[0]
    edge_w = w_hbm.shape[0] // mask_w.shape[0]
    z, row, q = lax.axis_index("sec"), lax.axis_index("row"), lax.axis_index("col")
    me = z * R + row
    core = row % 2
    xchip = row // 2
    p = xchip * S + z + (xchip % 2) * (S - 1 - 2 * z)
    sibling = (z, row + 1 - 2 * core, q)
    home = me // G

    def place(o):
        xo, zo = o // S, o % S
        return xo, zo + (xo % 2) * (S - 1 - 2 * zo)

    def wide_of(o, which=None):
        xo, zo = place(o)
        return zo * R + 2 * xo + (core if which is None else which)

    def row_of(w, r):
        zo, ro = w // R, w % R
        xo = ro // 2
        o = xo * S + zo + (xo % 2) * (S - 1 - 2 * zo)
        h, rest = r // half, r % half
        d = (p - o + nch) % nch if h == 0 else (o - p + nch) % nch
        index = (((d // near) * ways + h) * near + d % near) * 2 + ro % 2
        return pl.multiple_of(index * block_rows + rest * occ, occ)

    def device_at(o):
        xo, zo = place(o)
        return (zo, 2 * xo + core, q)

    after, before = device_at((p + 1) % nch), device_at((p + nch - 1) % nch)

    def origin(t, h):
        return (p + nch - t) % nch if h == 0 else (p + t) % nch

    def part(h):
        return pl.ds(h * half, half)

    def remote(src, dst, s, r, device):
        return pltpu.make_async_remote_copy(
            src_ref=src, dst_ref=dst, send_sem=s, recv_sem=r, device_id=device, device_id_type=MESH
        )

    def ring(t, h):
        piece = xa.at[wide_of(origin(t, h)), part(h)]
        return remote(piece, piece, ring_s.at[h, t], ring_r.at[h, t], after if h == 0 else before)

    def sib(t, h):
        piece = xa.at[wide_of(origin(t, h)), part(h)]
        return remote(piece, piece, sib_s.at[h, t], sib_r.at[h, t], sibling)

    def cross(t, h):
        w = wide_of(origin(t, h))
        goal = w // G
        slot = (q - goal - 1 + C) % C
        return goal, remote(
            xa.at[w, part(h)], xb.at[slot, w - goal * G, part(h)],
            y_s.at[h, t], y_r.at[slot, h, t], (z, row, goal),
        )

    def cross_in(t, h, slot):
        w = wide_of(origin(t, h))
        piece = xb.at[slot, w - (w // G) * G, part(h)]
        return w // G, piece

    barrier = pltpu.get_barrier_semaphore()

    def greet(d, carry):
        w, c = d // C, d % C

        @pl.when(d != me * C + q)
        def _():
            pl.semaphore_signal(barrier, inc=1, device_id=(w // R, w % R, c), device_id_type=MESH)

        return carry

    lax.fori_loop(0, W * C, greet, 0)
    own = pltpu.make_async_copy(x, xa.at[me], own_sem)
    own.start()

    def v_tile(s):
        size = va.shape[1]
        return pltpu.make_async_copy(v_hbm.at[pl.ds(s * size, size), :], va.at[s], tile_sem.at[0, s])

    def w_tile(s):
        size = wa.shape[2]
        return pltpu.make_async_copy(
            w_hbm.at[:, pl.ds(pl.multiple_of(s * size, size), size)], wa.at[s], tile_sem.at[1, s]
        )

    def load(s, carry):
        v_tile(s).start()
        w_tile(s).start()
        return carry

    own.wait()
    pl.semaphore_wait(barrier, W * C - 1)

    def cover(tile, s, rows, lanes, keep):
        keep = jnp.full((rows.size, lanes.size), keep.astype(jnp.float32)).astype(tile.dtype)
        tile[s, rows, lanes] = tile[s, rows, lanes] * keep

    def mask_tiles(s):
        strips, across = va.shape[1] // edge_v, va.shape[2] // edge_v
        v_tile(s).wait()
        for b in range(strips):
            for c in range(across):
                cover(va, s, pl.ds(b * edge_v, edge_v), pl.ds(c * edge_v, edge_v), mask_v[s * strips + b, c])
        strips, across = wa.shape[1] // edge_w, wa.shape[2] // edge_w
        w_tile(s).wait()
        for b in range(strips):
            for c in range(across):
                cover(wa, s, pl.ds(b * edge_w, edge_w), pl.ds(c * edge_w, edge_w), mask_w[b, s * across + c])

    def product(lhs, tile, s, transposed):
        dims = (((1,), (1 if transposed else 0,)), ((), ()))
        return lax.dot_general(lhs, tile[s], dims, preferred_element_type=jnp.float32)

    def step_a(far, tile, s, transposed):
        blocks = []
        for h in range(ways):
            for d in range(near):
                o = origin(far * near + d, h)
                for which in range(2):
                    piece = xa[wide_of(o, which), pl.ds(h * half, half), pl.ds(s, 1)]
                    blocks.append(piece.reshape(block_rows, vir))
        count = len(blocks) * block_rows
        span = pl.ds(far * count, count)
        acca[span, :] += product(jnp.concatenate(blocks, axis=0), tile, s, transposed)

    def unit_b(source, wl, h, slot, tile, transposed):
        for rest in range(half):
            r = h * half + rest
            lhs = source[r].reshape(tall * occ, vir)
            accb[slot] += product(lhs, tile, wl * wide + r, transposed)

    def own_units(t, tile, transposed):
        for h in range(ways):
            w = wide_of(origin(t, h), 0)

            @pl.when(w // G == q)
            def _():
                for which in range(2):
                    unit_b(xa.at[w + which], w + which - q * G, h, 0, tile, transposed)

    def cross_units(t, tile, transposed):
        for h in range(ways):
            w = wide_of(origin(t, h), 0)

            @pl.when(w // G == q)
            def _():
                for slot in range(C - 1):
                    wl = w + core - q * G
                    unit_b(xb.at[slot, wl], wl, h, 1 + slot, tile, transposed)
                    wl = w + 1 - core - q * G
                    piece = xb.at[slot, wl, part(h)]
                    remote(piece, piece, yb_s.at[slot, h, t], yb_r.at[slot, h, t], sibling).wait_recv()
                    unit_b(xb.at[slot, wl], wl, h, 1 + slot, tile, transposed)

    def gather(sweep, tile_a, tile_b, a_transposed):
        each = -(-tall // near)

        def slot_step(t, carry):
            for h in range(ways):
                @pl.when(t >= 1)
                def _():
                    ring(t - 1, h).wait_recv()

                @pl.when(t < nch - 1)
                def _():
                    ring(t, h).start()

                sib(t, h).start()
                goal, copy = cross(t, h)

                @pl.when(goal != q)
                def _():
                    copy.start()

            @pl.when(t >= 1)
            def _():
                for h in range(ways):
                    sib(t - 1, h).wait_recv()

            def work(n, carry):
                s = (t % near) * each + n

                @pl.when(s < tall)
                def _():
                    if sweep == 0:
                        @pl.when(t < near)
                        def _():
                            mask_tiles(s)

                    @pl.when(t >= near)
                    def _():
                        step_a(0, tile_a, s, a_transposed)

                return carry

            lax.fori_loop(0, each, work, 0)

            def pair(n, carry):
                d = 2 * (t - near) + n if sweep == 0 else t - 1

                @pl.when(jnp.logical_and(d >= 0, d < t))
                def _():
                    own_units(d, tile_b, not a_transposed)

                return carry

            lax.fori_loop(0, 2 if sweep == 0 else 1, pair, 0)
            return carry

        lax.fori_loop(0, nch, slot_step, 0)
        for h in range(ways):
            sib(nch - 1, h).wait_recv()
        own_units(nch - 1, tile_b, not a_transposed)

    def pass_on(t):
        for h in range(ways):
            for slot in range(C - 1):
                mine, piece = cross_in(t, h, slot)

                @pl.when(mine == q)
                def _():
                    remote(piece, piece, y_s.at[h, t], y_r.at[slot, h, t], sibling).wait_recv()
                    remote(piece, piece, yb_s.at[slot, h, t], yb_r.at[slot, h, t], sibling).start()

    def settle(t, carry):
        for h in range(ways):
            for slot in range(C - 1):
                mine, piece = cross_in(t, h, slot)

                @pl.when(mine == q)
                def _():
                    remote(piece, piece, yb_s.at[slot, h, t], yb_r.at[slot, h, t], sibling).wait_send()

            @pl.when(t < nch - 1)
            def _():
                ring(t, h).wait_send()

            sib(t, h).wait_send()
            goal, copy = cross(t, h)

            @pl.when(goal != q)
            def _():
                copy.wait_send()

        return carry

    def exchange_a(sweep, k):
        return remote(
            sa.at[k - 1], ra.at[sweep, C - 1 - k], ea_s.at[k - 1], ea_r.at[sweep, C - 1 - k], (z, row, (q + k) % C)
        )

    def exchange_b(sweep, k):
        w = (me + k) % W
        block = ((w // G - q + C) % C) * G + w % G
        return w, block, remote(
            sb.at[block], rb.at[sweep, q, me - home * G], eb_s.at[k], eb_r.at[sweep, q, me - home * G], (w // R, w % R, home)
        )

    def sweep_of(sweep, tile_a, tile_b, a_transposed):
        acca[...] = jnp.zeros_like(acca)
        accb[...] = jnp.zeros_like(accb)
        gather(sweep, tile_a, tile_b, a_transposed)

        each = -(-tall // nch)

        def arrivals(t, carry):
            def rest_a(n, carry):
                s = t * each + n

                @pl.when(s < tall)
                def _():
                    step_a(1, tile_a, s, a_transposed)

                return carry

            lax.fori_loop(0, each, rest_a, 0)
            pass_on(t)

            @pl.when(t >= 1)
            def _():
                cross_units(t - 1, tile_b, not a_transposed)

            return carry

        lax.fori_loop(0, nch, arrivals, 0)
        for k in range(1, C):
            def fill(wl, carry):
                for r in range(wide):
                    here = pl.ds(pl.multiple_of((wl * wide + r) * occ, occ), occ)
                    there = pl.ds(row_of(((q + k) % C) * G + wl, r), occ)
                    sa[k - 1, here, :] = acca[there, :].astype(sa.dtype)
                return carry

            lax.fori_loop(0, G, fill, 0)
            exchange_a(sweep, k).start()
        cross_units(nch - 1, tile_b, not a_transposed)
        lax.fori_loop(0, nch, settle, 0)
        if sweep == 0:
            for device in [after, before, sibling] + [(z, row, (q + k) % C) for k in range(1, C)]:
                pl.semaphore_signal(ready, inc=1, device_id=device, device_id_type=MESH)
        sb[...] = accb[...].reshape(sb.shape).astype(sb.dtype)

        def send(k, carry):
            w, block, copy = exchange_b(sweep, k)
            local = jnp.logical_and(w == me, home == q)

            @pl.when(local)
            def _():
                rb[sweep, q, me - home * G] = sb[block]

            @pl.when(jnp.logical_not(local))
            def _():
                copy.start()

            return carry

        lax.fori_loop(0, W, send, 0)
        for k in range(1, C):
            exchange_a(sweep, k).wait()

        def arrive(n, carry):
            c, wl = n // G, n % G

            @pl.when(jnp.logical_or(c != q, q * G + wl != me))
            def _():
                piece = rb.at[sweep, c, wl]
                remote(piece, piece, eb_s.at[0], eb_r.at[sweep, c, wl], sibling).wait_recv()

            return carry

        lax.fori_loop(0, W, arrive, 0)

        def sent(k, carry):
            w, block, copy = exchange_b(sweep, k)

            @pl.when(jnp.logical_not(jnp.logical_and(w == me, home == q)))
            def _():
                copy.wait_send()

            return carry

        lax.fori_loop(0, W, sent, 0)

        def assemble(wl, carry):
            for r in range(wide):
                place_r = wl * wide + r
                for s in range(wide):
                    lanes = pl.ds(s * vir, vir)
                    total = acca[pl.ds(row_of(q * G + wl, r), occ), lanes]
                    for slot in range(C - 1):
                        here = pl.ds(pl.multiple_of(place_r * occ, occ), occ)
                        total += ra[sweep, slot, here, lanes].astype(jnp.float32)
                    for c in range(C):
                        total += rb[sweep, c, wl, pl.ds(s * occ, occ), pl.ds(r * vir, vir)].astype(jnp.float32)
                    if sweep == 0:
                        total += drv[s, place_r].astype(jnp.float32)
                        value = total / (base[...] + (vir_a[me * wide + s] - occ_j[q * tall + place_r]))
                        out_one[s, place_r] = value
                        xa[me, s, place_r] = value.astype(xa.dtype)
                    else:
                        out_two[s, place_r] = total / (base[...] + (vir_a[q * tall + place_r] - occ_j[me * wide + s]))
            return carry

        lax.fori_loop(0, G, assemble, 0)
        if sweep == 0:
            pl.semaphore_wait(ready, C + 2)

    lax.fori_loop(0, tall, load, 0)
    for i in range(occ):
        base[pl.ds(i, 1), :] = vir_b[...] - occ_i[i]
    sweep_of(0, va, wa, False)
    sweep_of(1, wa, va, True)


def body(
    amps, driver, ladder_operator, ladder_block_mask, cycle_op, cycle_mask, occ_i, occ_j, vir_a, vir_b,
):
    S, R, C = lax.axis_size("sec"), lax.axis_size("row"), lax.axis_size("col")
    W = S * R
    G = W // C
    nch = W // 2
    occ, wide, tall, vir = amps.shape
    rows = W * wide * occ
    span = wide * vir
    x = jnp.transpose(amps, (1, 2, 0, 3))
    drv = jnp.transpose(driver, (2, 1, 0, 3))
    vmem = pl.BlockSpec(memory_space=pltpu.VMEM)
    smem = pl.BlockSpec(memory_space=pltpu.SMEM)
    hbm = pl.BlockSpec(memory_space=pl.ANY)
    dma = pltpu.SemaphoreType.DMA
    half = jnp.bfloat16
    result = jax.ShapeDtypeStruct((wide, tall, occ, vir), jnp.float32)
    one, two = pl.pallas_call(
        functools.partial(kernel, (S, R, C)),
        out_shape=(result, result),
        in_specs=[hbm, vmem, hbm, hbm, smem, smem, smem, smem, smem, vmem],
        out_specs=(vmem, vmem),
        scratch_shapes=[
            pltpu.VMEM((tall, vir, span), half),
            pltpu.VMEM((tall, span, vir), half),
            pltpu.VMEM((W, wide, tall, occ, vir), half),
            pltpu.VMEM((C - 1, G, wide, tall, occ, vir), half),
            pltpu.VMEM((rows, span), jnp.float32),
            pltpu.VMEM((C, tall * occ, span), jnp.float32),
            pltpu.VMEM((C - 1, rows // C, span), half),
            pltpu.VMEM((W, wide * occ, span), half),
            pltpu.VMEM((2, C - 1, rows // C, span), half),
            pltpu.VMEM((2, C, G, wide * occ, span), half),
            pltpu.VMEM((occ, vir), jnp.float32),
            dma((2, tall)),
            dma,
            dma((2, nch)),
            dma((2, nch)),
            dma((2, nch)),
            dma((2, nch)),
            dma((2, nch)),
            dma((C - 1, 2, nch)),
            dma((C - 1, 2, nch)),
            dma((C - 1, 2, nch)),
            dma((C - 1,)),
            dma((2, C - 1)),
            dma((W,)),
            dma((2, C, G)),
            pltpu.SemaphoreType.REGULAR,
        ],
        compiler_params=pltpu.CompilerParams(
            collective_id=0, has_side_effects=True, vmem_limit_bytes=63 * 1024 * 1024
        ),
    )(x, drv, ladder_operator, cycle_op, ladder_block_mask, cycle_mask, occ_i, occ_j, vir_a, vir_b[None])
    return jnp.transpose(one, (2, 1, 0, 3)), jnp.transpose(two, (2, 0, 1, 3))


def solution(mesh):
    placed = (
        P(None, ("sec", "row"), "col", None),
        P(None, "col", ("sec", "row"), None),
        P("col", ("sec", "row")),
        P("col", ("sec", "row")),
        P(("sec", "row"), "col"),
        P(("sec", "row"), "col"),
        P(),
        P(),
        P(),
        P(),
    )
    return jax.shard_map(
        body,
        mesh=mesh,
        in_specs=placed,
        out_specs=(P(None, "col", ("sec", "row"), None), P(None, ("sec", "row"), "col", None)),
        check_vma=False,
    )
```
